32 devices in a mesh: gx: 4 (over x, core), gy: 8 (over z, y).
Axes of the slice: x: 2, y: 2, z: 4, core: 2. Of those that a mesh axis runs over, the one named last changes fastest.
Arguments:
- reference_image: bfloat16 [32, 128, 1024], P(None, 'gx', 'gy'), may hold values from -6 to 6
- moving_image: float32 [44, 128, 1024], P(None, 'gx', 'gy'), may hold values from -6 to 6
- image_gradient: bfloat16 [3, 32, 128, 1024], P(None, None, 'gx', 'gy'), may hold values from -1.5 to 1.5
- voxel_shift: int32 [3, 4, 16, 128], P(None, None, 'gx', 'gy'), may hold values from -6 to 5
- subvoxel: float32 [3, 4, 16, 128], P(None, None, 'gx', 'gy'), may hold values from 0 to 1
Outputs:
- increment: float32 [3, 5, 16, 128], P(None, None, 'gx', 'gy')
- cg_residual: float32 [3, 5, 16, 128], P(None, None, 'gx', 'gy')
The draws below stay inside these ranges and needn't reach their ends.
All inputs are finite; a program needn't handle non-finite values.
Results may differ from the reference program's by a relative error of at most 0.0003.
Values sent between devices are 32-bit elements; how exact they have to be, the bound alone decides.
A program may use at most 128 MiB of HBM per device.

```python
import jax
import jax.numpy as jnp
from jax import lax

CZ = 32
ELEM = 8
HW = 6
ITERS = 3
NX = 128
NY = 1024
GZ = 44
NZE = 4
NXE = 16
NYE = 128


def plant(array, key, least, high):
    place = [jax.random.randint(jax.random.fold_in(key, axis), (), 0, length) for axis, length in enumerate(array.shape)]
    widest = array.shape.index(max(array.shape))
    next_to = place[:widest] + [(place[widest] + 1) % array.shape[widest]] + place[widest + 1:]
    return array.at[tuple(place)].set(least).at[tuple(next_to)].set(high)


def steps_of(stream_key, shape, split, least, top_value):
    def one(position, shards_of):
        draws = jax.random.uniform(jax.random.fold_in(jax.random.fold_in(stream_key, 6), position), (shards_of,), jnp.float32, least / len(split), top_value / len(split))
        return jnp.repeat(jnp.exp(draws), shape[position] // shards_of).reshape((-1,) + (1,) * (len(shape) - position - 1))

    gain = one(*split[0])
    for cut in split[1:]:
        gain = gain * one(*cut)
    return gain


def centred(own_key, extent, width, limit, cuts=(), kind=jnp.bfloat16):
    values = width * jax.random.normal(own_key, extent, jnp.float32)
    if cuts:
        values = values * steps_of(own_key, extent, cuts, -0.22, 0.18)
    return jnp.clip(values, -limit, limit).astype(kind)


def setup_inputs(seed: int = 0) -> dict:
    key_list = jax.random.split(jax.random.key(seed), 6)
    reference_image = centred(key_list[0], (CZ, NX, NY), 1.0, 6.0, ((1, 4), (2, 8)))
    moving_image = centred(key_list[1], (GZ, NX, NY), 1.0, 6.0, ((1, 4), (2, 8)), jnp.float32)
    image_gradient = centred(key_list[2], (3, CZ, NX, NY), 0.25, 1.5, ((2, 4), (3, 8)))
    voxel_shift = plant(jax.random.randint(key_list[3], (3, NZE, NXE, NYE), -HW, HW), jax.random.fold_in(key_list[3], 1), -HW, HW - 1).astype(jnp.int32)
    subvoxel = jnp.clip(1.0 * jax.random.uniform(key_list[4], (3, NZE, NXE, NYE), jnp.float32) ** steps_of(key_list[4], (3, NZE, NXE, NYE), ((2, 4), (3, 8)), -0.2, 0.2), 0.0, 1.0)
    return dict(reference_image=reference_image, moving_image=moving_image, image_gradient=image_gradient, voxel_shift=voxel_shift, subvoxel=subvoxel)


ridge_weight = 2.0


def linear_basis():
    centres = (jnp.arange(ELEM, dtype=jnp.float32) + 0.5) / ELEM
    return jnp.stack([1.0 - centres, centres])


def corner_sides():
    return [(side_z, side_x, side_y) for side_z in (0, 1) for side_x in (0, 1) for side_y in (0, 1)]


def element_view(volume):
    extent_z, extent_x, extent_y = volume.shape
    return volume.reshape(extent_z // ELEM, ELEM, extent_x // ELEM, ELEM, extent_y // ELEM, ELEM)


def element_stiffness(gradient):
    shape_basis = linear_basis()
    basis_pairs = shape_basis[:, None, :] * shape_basis[None, :, :]
    blocks = {}
    for first_comp in range(3):
        for second_comp in range(first_comp, 3):
            product = gradient[first_comp].astype(jnp.float32) * gradient[second_comp].astype(jnp.float32)
            summed = jnp.einsum("zixjyl,pqi,rsj,tul->prtqsuzxy", element_view(product), basis_pairs, basis_pairs, basis_pairs, precision=lax.Precision.HIGHEST)
            blocks[(first_comp, second_comp)] = summed.reshape(8, 8, -1)
            blocks[(second_comp, first_comp)] = blocks[(first_comp, second_comp)]
    stiff_rows = []
    for first_comp in range(3):
        stiff_rows.append(jnp.stack([blocks[(first_comp, second_comp)] for second_comp in range(3)], axis=2))
    return jnp.stack(stiff_rows, axis=1)


def element_load(image, gradient, warped):
    shape_basis = linear_basis()
    mismatch = image.astype(jnp.float32) - warped
    load_terms = []
    for component in range(3):
        weighted = gradient[component].astype(jnp.float32) * mismatch
        summed = jnp.einsum("zixjyl,pi,qj,rl->pqrzxy", element_view(weighted), shape_basis, shape_basis, shape_basis, precision=lax.Precision.HIGHEST)
        load_terms.append(summed.reshape(8, -1))
    return jnp.stack(load_terms, axis=1)


def warp_blocks(padded, voxel_shift, subvoxel, x_anchor, y_anchor):
    count_z = voxel_shift.shape[1]
    count_x = voxel_shift.shape[2]
    count_y = voxel_shift.shape[3]
    index_z = jnp.arange(count_z, dtype=jnp.int32)[:, None, None] * ELEM
    index_x = jnp.arange(count_x, dtype=jnp.int32)[None, :, None] * ELEM + x_anchor
    index_y = jnp.arange(count_y, dtype=jnp.int32)[None, None, :] * ELEM + y_anchor
    start_z = (index_z + voxel_shift[0] + HW).astype(jnp.int32).reshape(-1)
    start_x = (index_x + voxel_shift[1] + HW).astype(jnp.int32).reshape(-1)
    start_y = (index_y + voxel_shift[2] + HW).astype(jnp.int32).reshape(-1)

    def cut_block(corner_z, corner_x, corner_y):
        return lax.dynamic_slice(padded, (corner_z, corner_x, corner_y), (ELEM + 1, ELEM + 1, ELEM + 1))

    gathered = jax.vmap(cut_block, out_axes=3)(start_z, start_x, start_y)
    weight_z = subvoxel[0].reshape(-1)
    weight_x = subvoxel[1].reshape(-1)
    weight_y = subvoxel[2].reshape(-1)
    along_z = (1.0 - weight_z) * gathered[:ELEM] + weight_z * gathered[1:]
    along_x = (1.0 - weight_x) * along_z[:, :ELEM] + weight_x * along_z[:, 1:]
    along_y = (1.0 - weight_y) * along_x[:, :, :ELEM] + weight_y * along_x[:, :, 1:]
    shaped = along_y.reshape(ELEM, ELEM, ELEM, count_z, count_x, count_y)
    return shaped.transpose(3, 0, 4, 1, 5, 2).reshape(count_z * ELEM, count_x * ELEM, count_y * ELEM)


def nodes_to_elements(nodal_field, count_z, count_x, count_y):
    picked = [nodal_field[:, side_z:side_z + count_z, side_x:side_x + count_x, side_y:side_y + count_y] for (side_z, side_x, side_y) in corner_sides()]
    return jnp.stack(picked).reshape(8, 3, -1)


def elements_to_nodes(element_terms, count_z, count_x, count_y):
    shaped = element_terms.reshape(8, 3, count_z, count_x, count_y)
    nodal_sum = jnp.zeros((3, count_z + 1, count_x + 1, count_y + 1), jnp.float32)
    for corner_index, (side_z, side_x, side_y) in enumerate(corner_sides()):
        nodal_sum = nodal_sum + jnp.pad(shaped[corner_index], ((0, 0), (side_z, 1 - side_z), (side_x, 1 - side_x), (side_y, 1 - side_y)))
    return nodal_sum


def element_product(stiffness, element_values):
    return jnp.sum(stiffness * element_values[None, None], axis=(2, 3))


def reference(reference_image, moving_image, image_gradient, voxel_shift, subvoxel):
    count_z = CZ // ELEM
    count_x = NX // ELEM
    count_y = NY // ELEM
    padded = jnp.pad(moving_image, ((0, 0), (HW, HW), (HW, HW)))
    image_rows = reference_image.reshape(CZ, count_x, ELEM, NY).transpose(1, 0, 2, 3)
    gradient_rows = image_gradient.reshape(3, CZ, count_x, ELEM, NY).transpose(2, 0, 1, 3, 4)
    shift_rows = voxel_shift.transpose(2, 0, 1, 3)[:, :, :, None, :]
    frac_rows = subvoxel.transpose(2, 0, 1, 3)[:, :, :, None, :]
    anchors = jnp.arange(count_x, dtype=jnp.int32) * ELEM

    def one_row(inputs):
        image_row, gradient_row, shift_row, frac_row, anchor = inputs
        warped = warp_blocks(padded, shift_row, frac_row, anchor, 0)
        return element_stiffness(gradient_row), element_load(image_row, gradient_row, warped)

    stiff_map, load_map = lax.map(one_row, (image_rows, gradient_rows, shift_rows, frac_rows, anchors))
    stiffness = jnp.moveaxis(stiff_map.reshape(count_x, 8, 3, 8, 3, count_z, count_y), 0, 5).reshape(8, 3, 8, 3, -1)
    load_flat = jnp.moveaxis(load_map.reshape(count_x, 8, 3, count_z, count_y), 0, 3).reshape(8, 3, -1)
    load_nodes = elements_to_nodes(load_flat, count_z, count_x, count_y)

    def apply_operator(nodal_field):
        element_values = nodes_to_elements(nodal_field, count_z, count_x, count_y)
        return elements_to_nodes(element_product(stiffness, element_values), count_z, count_x, count_y) + ridge_weight * nodal_field

    solution = jnp.zeros_like(load_nodes)
    residual = load_nodes
    direction = load_nodes
    norm_now = jnp.sum(residual * residual)
    for iteration in range(ITERS):
        image_dir = apply_operator(direction)
        step_length = norm_now / jnp.sum(direction * image_dir)
        solution = solution + step_length * direction
        residual = residual - step_length * image_dir
        norm_next = jnp.sum(residual * residual)
        direction = residual + (norm_next / norm_now) * direction
        norm_now = norm_next
    return solution[:, :, :count_x, :count_y], residual[:, :, :count_x, :count_y]
```

```python
import functools

import jax
import jax.numpy as jnp
import numpy as np
from jax import lax
from jax.experimental import pallas as pl
from jax.experimental.pallas import tpu as pltpu
from jax.sharding import PartitionSpec as P

ELEM = 8
HW = 6
ITERS = 3
LANES = 128
ROWS = 8
RIDGE = 2.0
TAPS = 2 * HW + 1
COMP = {(0, 0): 0, (0, 1): 1, (0, 2): 2, (1, 1): 3, (1, 2): 4, (2, 2): 5}
MESH = pl.DeviceIdType.MESH


def phi():
    centre = (np.arange(ELEM, dtype=np.float64) + 0.5) / ELEM
    return np.stack([1.0 - centre, centre])


def placed_weights(classes, count_x, count_y, stride):
    size_y = count_y * ELEM
    out = np.zeros((count_x, size_y, len(classes), LANES), np.float32)
    for ex in range(count_x):
        for y in range(size_y):
            for c, w in enumerate(classes):
                out[ex, y, c, ex * stride + y // ELEM] = w[y % ELEM]
    return out.reshape(count_x * size_y, len(classes) * LANES)


def exact_dot(values, weights):
    total = None
    rest = values
    for _ in range(3):
        part = rest.astype(jnp.bfloat16)
        rest = rest - part.astype(jnp.float32)
        term = jnp.dot(part, weights, preferred_element_type=jnp.float32)
        total = term if total is None else total + term
    return total


def padded_2(cells, sides, width):
    for axis, dim in sides:
        count = lax.axis_size(axis)
        ends = count - 1
        head = lax.slice_in_dim(cells, 0, width, axis=dim)
        tail = lax.slice_in_dim(cells, cells.shape[dim] - width, cells.shape[dim], axis=dim)
        cells = jnp.concatenate(
            [
                lax.ppermute(tail, axis, [(i, (i + 1) % count) for i in range(ends)]),
                cells,
                lax.ppermute(head, axis, [((i + 1) % count, i) for i in range(ends)]),
            ],
            axis=dim,
        )
    return cells


def element_kernel(dims, pad_ref, image_ref, grad_ref, shift_ref, frac_ref, wx_ref, bs_ref, bl_ref,
                   stiff_ref, load_ref, rolled, ysum, xsum, vs, vl):
    count_z, count_x, size_y = dims
    p = phi()
    pairs = [p[0] * p[0], p[0] * p[1], p[1] * p[1]]
    span = ELEM + TAPS - 1
    depth = pad_ref.shape[0]
    f32 = jnp.float32

    @pl.loop(0, depth)
    def _(z):
        row = pad_ref[z]
        for d in range(TAPS):
            rolled[d, z] = row[:, d : d + size_y]

    vs[...] = jnp.zeros_like(vs)
    vl[...] = jnp.zeros_like(vl)

    def taps(axis, row):
        s = shift_ref[axis, pl.ds(row, 1), :] + HW
        w = frac_ref[axis, pl.ds(row, 1), :]
        zero = jnp.zeros_like(w)
        return [
            jnp.where(s == d, 1.0 - w, zero) + jnp.where(s == d - 1, w, zero) for d in range(TAPS)
        ]

    for ez in range(count_z):

        @pl.loop(0, count_x)
        def _(ex, ez=ez):
            row = ez * count_x + ex
            z0 = ez * ELEM
            x0 = pl.multiple_of(ex * ELEM, ELEM)
            chunk = 4
            wy = [jnp.broadcast_to(t, (ELEM, size_y)) for t in taps(2, row)]
            for c in range(0, span, chunk):
                for t in range(3):
                    acc = None
                    for d in range(TAPS):
                        v = wy[d][None] * rolled[
                            d, pl.ds(z0 + c, chunk), pl.ds(x0 + t * ELEM, ELEM), :
                        ]
                        acc = v if acc is None else acc + v
                    ysum[c : c + chunk, t * ELEM : (t + 1) * ELEM, :] = acc
            wt = [jnp.broadcast_to(t, (ELEM, size_y)) for t in taps(1, row)]
            for c in range(0, span, chunk):
                acc = None
                for d in range(TAPS):
                    v = wt[d][None] * ysum[c : c + chunk, d : d + ELEM, :]
                    acc = v if acc is None else acc + v
                xsum[c : c + chunk] = acc
            wz = [jnp.broadcast_to(t, (ELEM, size_y)) for t in taps(0, row)]
            warped = None
            for d in range(TAPS):
                v = wz[d][None] * xsum[d : d + ELEM]
                warped = v if warped is None else warped + v
            image = image_ref[pl.ds(z0, ELEM), pl.ds(x0, ELEM), :].astype(f32)
            mismatch = image - warped
            grads = [
                grad_ref[k, pl.ds(z0, ELEM), pl.ds(x0, ELEM), :].astype(f32) for k in range(3)
            ]

            def along_z(volume, weights):
                acc = None
                for i in range(ELEM):
                    v = float(weights[i]) * volume[i]
                    acc = v if acc is None else acc + v
                return acc

            for k in range(3):
                weighted = grads[k] * mismatch
                for a in range(2):
                    plane = along_z(weighted, p[a])
                    for b in range(2):
                        line = jnp.sum(plane * wx_ref[3 + b], axis=0, keepdims=True)
                        vl[(k * 2 + a) * 2 + b, ex, ez : ez + 1, :] = line
            for (k, k2), m in COMP.items():
                product = grads[k] * grads[k2]
                for a in range(3):
                    plane = along_z(product, pairs[a])
                    for b in range(3):
                        line = jnp.sum(plane * wx_ref[b], axis=0, keepdims=True)
                        vs[(m * 3 + a) * 3 + b, ex, ez : ez + 1, :] = line

    def side_by_side(ref, start, count):
        return jnp.concatenate(
            [
                ref[start : start + count, ex].reshape(count * ROWS, size_y)
                for ex in range(count_x)
            ],
            axis=1,
        )

    for m in range(6):
        block = side_by_side(vs, m * 9, 9)
        got = exact_dot(block, bs_ref[...])
        for a in range(3):
            for b in range(3):
                for c in range(3):
                    g = (a * 3 + b) * ROWS
                    stiff_ref[m, a, b, c] = got[g : g + ROWS, c * LANES : (c + 1) * LANES]
    got = exact_dot(side_by_side(vl, 0, 12), bl_ref[...])
    for k in range(3):
        for a in range(2):
            for b in range(2):
                for c in range(2):
                    g = ((k * 2 + a) * 2 + b) * ROWS
                    load_ref[k, a, b, c] = got[g : g + ROWS, c * LANES : (c + 1) * LANES]


def solve_kernel(dims, stiff_ref, load_ref, out_u, out_r, send_x, send_y, got_x, got_y,
                 ssem_x, ssem_y, rsem_x, rsem_y):
    count_x, count_y, stride, nx, ny = dims
    mx, my = lax.axis_index("gx"), lax.axis_index("gy")

    barrier = pltpu.get_barrier_semaphore()
    for d in range(1, nx):
        pl.semaphore_signal(barrier, inc=1, device_id=(lax.rem(mx + d, nx), my), device_id_type=MESH)
    for d in range(1, ny):
        pl.semaphore_signal(barrier, inc=1, device_id=(mx, lax.rem(my + d, ny)), device_id_type=MESH)

    lane = lax.broadcasted_iota(jnp.int32, (ROWS, LANES), 1)
    ix = lane // stride
    iy = lane % stride

    def ones(cond):
        return jnp.where(cond, 1.0, 0.0).astype(jnp.float32)

    def flag(cond):
        return jnp.where(cond, 1.0, 0.0).astype(jnp.float32)

    not_first_x, not_last_x = flag(mx > 0), flag(mx < nx - 1)
    not_first_y, not_last_y = flag(my > 0), flag(my < ny - 1)
    low_x, high_x = ones(ix == 0) * not_first_x, ones(ix == count_x) * not_last_x
    node = ones(ix <= count_x) * ones(iy <= count_y)
    low_y = node * ones(iy == 0) * not_first_y
    high_y = node * ones(iy == count_y) * not_last_y
    owner = node * (1.0 - high_x) * (1.0 - high_y)

    def rolled(v, rows, lanes):
        if rows % ROWS:
            v = pltpu.roll(v, rows % ROWS, 0)
        if lanes % LANES:
            v = pltpu.roll(v, lanes % LANES, 1)
        return v

    sides = [(a, b, c) for a in (0, 1) for b in (0, 1) for c in (0, 1)]

    def scatter(terms):
        out = []
        for k in range(3):
            acc = None
            for a, b, c in sides:
                v = rolled(terms(k, a, b, c), a, b * stride + c)
                acc = v if acc is None else acc + v
            out.append(acc)
        return out

    def stage(rnd, field, tile, axis):
        n, me = (nx, mx) if axis == 0 else (ny, my)
        send, got, ssem, rsem = (
            (send_x, got_x, ssem_x, rsem_x) if axis == 0 else (send_y, got_y, ssem_y, rsem_y)
        )
        for k in range(3):
            send[rnd, k] = field[k]
        send[rnd, 3] = tile if tile is not None else jnp.zeros_like(field[0])
        copies = []
        order = [1, n - 1] + list(range(2, n - 1))
        for d in order:
            near = d in (1, n - 1)
            if tile is None and not near:
                continue
            to = lax.rem(me + d, n)
            target = (to, my) if axis == 0 else (mx, to)
            src = send.at[rnd] if near else send.at[rnd, 3]
            dst = got.at[rnd, d - 1] if near else got.at[rnd, d - 1, 3]
            copy = pltpu.make_async_remote_copy(
                src_ref=src, dst_ref=dst, send_sem=ssem.at[rnd, d - 1],
                recv_sem=rsem.at[rnd, d - 1], device_id=target, device_id_type=MESH,
            )
            copy.start()
            copies.append((d, copy))
        for d, copy in copies:
            copy.wait_recv()
        hop = count_x * stride if axis == 0 else count_y
        low, high = (low_x, high_x) if axis == 0 else (low_y, high_y)
        out = []
        for k in range(3):
            from_low = rolled(got[rnd, 0, k], 0, -hop)
            from_high = rolled(got[rnd, n - 2, k], 0, hop)
            out.append(field[k] + low * from_low + high * from_high)
        if tile is not None:
            for d in range(1, n):
                tile = tile + got[rnd, d - 1, 3]
        return out, tile, [copy for _, copy in copies]

    pending = []

    def exchange(rnd, field, tile):
        field, tile, first = stage(rnd, field, tile, 0)
        field, tile, second = stage(rnd, field, tile, 1)
        pending.extend(first + second)
        return field, tile

    load = scatter(lambda k, a, b, c: load_ref[k, a, b, c])
    pl.semaphore_wait(barrier, nx - 1 + ny - 1)
    r, _ = exchange(0, load, None)
    row = lax.broadcasted_iota(jnp.int32, (ROWS, LANES), 0)
    u = p = q = rr = alpha = None
    for it in range(ITERS):
        force = None
        inputs = {}
        for a, b, c in sides:
            for k2 in range(3):
                v = rolled(r[k2], -a, -(b * stride + c))
                inputs[k2, a, b, c] = v
                block = jnp.stack([
                    stiff_ref[COMP[min(k, k2), max(k, k2)], a : a + 2, b : b + 2, c : c + 2]
                    for k in range(3)
                ])
                term = block * v[None, None, None, None]
                force = term if force is None else force + term
        energy = None
        for (k, a, b, c), v in inputs.items():
            term = force[k, a, b, c] * v
            energy = term if energy is None else energy + term
        square = (r[0] * r[0] + r[1] * r[1] + r[2] * r[2]) * owner
        tile = jnp.where(
            row == 0,
            jnp.sum(square, axis=0, keepdims=True),
            jnp.where(row == 1, jnp.sum(energy, axis=0, keepdims=True), 0.0),
        )
        w, total = exchange(1 + it, scatter(lambda k, a, b, c: force[k, a, b, c]), tile)
        w = [w[k] + RIDGE * r[k] for k in range(3)]
        sums = jnp.sum(total, axis=1, keepdims=True)
        new = sums[0:1]
        image = sums[1:2] + RIDGE * new
        if it == 0:
            p, q = r, w
            alpha = new / image
            u = [alpha * p[k] for k in range(3)]
        else:
            beta = new / rr
            alpha_next = new / (image - beta * new / alpha)
            p = [r[k] + beta * p[k] for k in range(3)]
            q = [w[k] + beta * q[k] for k in range(3)]
            alpha = alpha_next
            u = [u[k] + alpha * p[k] for k in range(3)]
        r = [r[k] - alpha * q[k] for k in range(3)]
        rr = new
    for copy in pending:
        copy.wait_send()
    for k in range(3):
        out_u[k] = u[k]
        out_r[k] = r[k]


def body(nx, ny, reference_image, moving_image, image_gradient, voxel_shift, subvoxel):
    f32 = jnp.float32
    _, count_z, count_x, count_y = voxel_shift.shape
    size_y = count_y * ELEM
    stride = count_y + 8
    padded = padded_2(moving_image, (("gx", 1), ("gy", 2)), HW)
    extra_x = -padded.shape[1] % 8 + (8 if padded.shape[1] % 8 == 0 else 0)
    padded = jnp.pad(padded, ((0, 0), (0, extra_x), (0, 2 * LANES - padded.shape[2])))
    rows = count_z * count_x
    shift = jnp.repeat(voxel_shift.reshape(3, rows, count_y), ELEM, axis=2)
    frac = jnp.repeat(subvoxel.reshape(3, rows, count_y), ELEM, axis=2)
    p = phi()
    pairs = [p[0] * p[0], p[0] * p[1], p[1] * p[1]]
    wx = np.broadcast_to(
        np.stack(pairs + [p[0], p[1]]).astype(np.float32)[:, :, None], (5, ELEM, size_y)
    )
    bs = placed_weights(pairs, count_x, count_y, stride)
    bl = placed_weights([p[0], p[1]], count_x, count_y, stride)
    span = ELEM + TAPS - 1
    vmem = pl.BlockSpec(memory_space=pltpu.VMEM)
    stiff, load = pl.pallas_call(
        functools.partial(element_kernel, (count_z, count_x, size_y)),
        out_shape=[
            jax.ShapeDtypeStruct((6, 3, 3, 3, ROWS, LANES), f32),
            jax.ShapeDtypeStruct((3, 2, 2, 2, ROWS, LANES), f32),
        ],
        in_specs=[vmem] * 8,
        out_specs=[vmem] * 2,
        scratch_shapes=[
            pltpu.VMEM((TAPS, padded.shape[0], padded.shape[1], size_y), f32),
            pltpu.VMEM((span, 3 * ELEM, size_y), f32),
            pltpu.VMEM((span, ELEM, size_y), f32),
            pltpu.VMEM((54, count_x, ROWS, size_y), f32),
            pltpu.VMEM((12, count_x, ROWS, size_y), f32),
        ],
        compiler_params=pltpu.CompilerParams(vmem_limit_bytes=48 * 1024 * 1024),
        name="elements",
    )(padded, reference_image, image_gradient, shift, frac, jnp.asarray(wx), jnp.asarray(bs, jnp.bfloat16),
      jnp.asarray(bl, jnp.bfloat16))
    rounds = ITERS + 1
    dma = pltpu.SemaphoreType.DMA
    u, r = pl.pallas_call(
        functools.partial(solve_kernel, (count_x, count_y, stride, nx, ny)),
        out_shape=[jax.ShapeDtypeStruct((3, ROWS, LANES), f32)] * 2,
        in_specs=[vmem] * 2,
        out_specs=[vmem] * 2,
        scratch_shapes=[
            pltpu.VMEM((rounds, 4, ROWS, LANES), f32),
            pltpu.VMEM((rounds, 4, ROWS, LANES), f32),
            pltpu.VMEM((rounds, nx - 1, 4, ROWS, LANES), f32),
            pltpu.VMEM((rounds, ny - 1, 4, ROWS, LANES), f32),
            dma((rounds, nx - 1)),
            dma((rounds, ny - 1)),
            dma((rounds, nx - 1)),
            dma((rounds, ny - 1)),
        ],
        compiler_params=pltpu.CompilerParams(
            collective_id=0, has_side_effects=True, vmem_limit_bytes=32 * 1024 * 1024
        ),
        name="solve",
    )(stiff, load)

    def unpack(field):
        grid = field[:, : count_z + 1, : count_x * stride]
        return grid.reshape(3, count_z + 1, count_x, stride)[..., :count_y]

    return unpack(u), unpack(r)


def solution(mesh):
    placed = (
        P(None, "gx", "gy"),
        P(None, "gx", "gy"),
        P(None, None, "gx", "gy"),
        P(None, None, "gx", "gy"),
        P(None, None, "gx", "gy"),
    )
    return jax.shard_map(
        functools.partial(body, mesh.shape["gx"], mesh.shape["gy"]),
        mesh=mesh,
        in_specs=placed,
        out_specs=(P(None, None, "gx", "gy"), P(None, None, "gx", "gy")),
        check_vma=False,
    )
```
